32 devices in a mesh: fsdp: 4 (over y, x), tp: 4 (over z), rep: 2 (over core).
Axes of the slice: x: 2, y: 2, z: 4, core: 2. Of those that a mesh axis runs over, the one named last changes fastest.
Arguments:
- hidden_in: bfloat16 [2, 1024, 5120], P(None, ('fsdp', 'rep')), may hold values from -6 to 6
- norm_gain: float32 [5120], replicated, may hold values from 0.1 to 1.9
- q_weight: bfloat16 [1024, 5120], P('tp'), may hold values from -0.078125 to 0.078125
- q_bias: bfloat16 [1024], P('tp'), may hold values from -3 to 3
- kv_weight: bfloat16 [2, 256, 5120], P(None, 'tp'), may hold values from -0.078125 to 0.078125
- kv_bias: bfloat16 [2, 256], P(None, 'tp'), may hold values from -3 to 3
- o_weight: bfloat16 [5120, 1024], P(None, 'tp'), may hold values from -0.1875 to 0.1875
- q_delta: bfloat16 [1024, 5120], P('tp', ('fsdp', 'rep')), may hold values from -4 to 4
- q_scale_exp: int32 [1024, 160], P('tp', ('fsdp', 'rep')), may hold values from -9 to -5
- kv_delta: bfloat16 [2, 256, 5120], P(None, 'tp', ('fsdp', 'rep')), may hold values from -4 to 4
- kv_scale_exp: int32 [2, 256, 160], P(None, 'tp', ('fsdp', 'rep')), may hold values from -9 to -5
- o_delta: bfloat16 [5120, 1024], P(('fsdp', 'rep'), 'tp'), may hold values from -4 to 4
- o_scale_exp: int32 [5120, 32], P(('fsdp', 'rep'), 'tp'), may hold values from -9 to -5
- key_cache: bfloat16 [1024, 4, 32, 128], P(('fsdp', 'rep'), 'tp'), may hold values from -2000 to 2000
- value_cache: bfloat16 [1024, 4, 32, 128], P(('fsdp', 'rep'), 'tp'), may hold values from -5 to 5
- cache_lengths: int32 [1024], P(('fsdp', 'rep')), may hold values from 1 to 64
Outputs:
- decoded: bfloat16 [2, 1024, 5120], P(None, ('fsdp', 'rep'), 'tp')
The draws below stay inside these ranges and needn't reach their ends.
All inputs are finite; a program needn't handle non-finite values.
Results may differ from the reference program's by a relative error of at most 0.009.
The reference program's roundings to bfloat16 on the way count: a program that leaves them out, or rounds other values in their place, can miss the bound.
Values may be sent and summed in bfloat16 or wider, within the bound.
No kernel may reach another device: no remote copies, remote signals or barrier semaphores. Data moves between devices by JAX's collectives and lax.ppermute only.
A program may use at most 128 MiB of HBM per device.

```python
import jax
import jax.numpy as jnp
from jax import lax

D = 5120
HD = 128
QH = 8
KVH = 2
BLOCK = 32
STEPS = 2
CTX = 64
QW = 1024
KVW = 256
BATCH = 1024


def draw_key_cache(key, part):
    key = jax.random.fold_in(key, 7)
    shape_full = (BATCH, 2 * KVH, CTX // 2, HD)
    normal_keys = jnp.clip(jax.random.normal(key, shape_full, jnp.float32), -4.5, 4.5)
    return normal_keys.astype(jnp.bfloat16)


def with_ends(result, rng, smallest, high):
    longest = result.shape.index(max(result.shape))
    spots = []
    for shift in (0, 1):
        where = [jax.random.randint(jax.random.fold_in(rng, axis), (), 0, length) for axis, length in enumerate(result.shape)]
        where[longest] = (where[longest] + shift) % result.shape[longest]
        spots.append(tuple(where))
    return result.at[spots[0]].set(smallest).at[spots[1]].set(high)


def steps_of(stream_key, extent, shards, low, top_value):
    level, own = 1.0, jax.random.fold_in(stream_key, 6)
    for axis_at, shards_of in shards:
        draws = jnp.exp(jax.random.uniform(jax.random.fold_in(own, axis_at), (shards_of,), jnp.float32, low / len(shards), top_value / len(shards)))
        level = level * jnp.repeat(draws, extent[axis_at] // shards_of).reshape([-1 if axis == axis_at else 1 for axis in range(len(extent))])
    return level


def noise(key, dims, deviation, bound, split=(), held_as=jnp.bfloat16):
    result = deviation * jax.random.normal(key, dims, jnp.float32)
    if split:
        result = result * steps_of(key, dims, split, -0.22, 0.18)
    return jnp.clip(result, -bound, bound).astype(held_as)


def setup_inputs(seed: int = 0) -> dict:
    splits = jax.random.split(jax.random.key(seed), 17)
    return {
        "hidden_in": noise(splits[0], (STEPS, BATCH, D), 1.0, 6.0, ((1, 8),)),
        "norm_gain": jnp.clip(1.0 + 0.18 * jax.random.normal(splits[1], (D,), jnp.float32), 0.1, 1.9),
        "q_weight": noise(splits[2], (QW, D), D ** -0.5, 0.078125, ((0, 4),)),
        "q_bias": noise(splits[3], (QW,), 0.5, 3.0, ((0, 4),)),
        "kv_weight": noise(splits[4], (2, KVW, D), D ** -0.5, 0.078125, ((1, 4),)),
        "kv_bias": noise(splits[5], (2, KVW), 0.5, 3.0, ((1, 4),)),
        "o_weight": noise(splits[6], (D, QW), QW ** -0.5, 0.1875, ((1, 4),)),
        "q_delta": noise(splits[7], (QW, D), 1.0, 4.0, ((0, 4), (1, 8))),
        "q_scale_exp": with_ends(jax.random.randint(splits[8], (QW, D // BLOCK), -9, -4), jax.random.fold_in(splits[8], 1), -9, (-4) - 1).astype(jnp.int32),
        "kv_delta": noise(splits[9], (2, KVW, D), 1.0, 4.0, ((1, 4), (2, 8))),
        "kv_scale_exp": with_ends(jax.random.randint(splits[10], (2, KVW, D // BLOCK), -9, -4), jax.random.fold_in(splits[10], 1), -9, (-4) - 1).astype(jnp.int32),
        "o_delta": noise(splits[11], (D, QW), 1.0, 4.0, ((0, 8), (1, 4))),
        "o_scale_exp": with_ends(jax.random.randint(splits[12], (D, QW // BLOCK), -9, -4), jax.random.fold_in(splits[12], 1), -9, (-4) - 1).astype(jnp.int32),
        "key_cache": draw_key_cache(jax.random.fold_in(splits[16], 71), 0),
        "value_cache": noise(splits[14], (BATCH, 2 * KVH, CTX // 2, HD), 1.0, 5.0, ((0, 8), (1, 4))),
        "cache_lengths": with_ends(jax.random.randint(splits[15], (BATCH,), 1, CTX + 1), jax.random.fold_in(splits[15], 1), 1, CTX).astype(jnp.int32),
    }


def refresh(base_matrix, delta, exponents):
    factor = jnp.exp2(exponents.astype(jnp.float32))
    full_shape = delta.shape
    blocks = delta.astype(jnp.float32).reshape(full_shape[:-1] + (full_shape[-1] // BLOCK, BLOCK))
    change = (blocks * factor[..., None]).reshape(full_shape)
    return (base_matrix.astype(jnp.float32) + change).astype(jnp.bfloat16)

def rms_norm(hidden, gain_vector):
    values = hidden.astype(jnp.float32)
    inv_root = lax.rsqrt(lax.optimization_barrier(jnp.mean(values * values, axis=-1, keepdims=True)) + 1e-06)
    return (values * inv_root * gain_vector).astype(jnp.bfloat16)

def rotate(vectors, position):
    half_size = vectors.shape[-1] // 2
    frequency = 1000000.0 ** (-jnp.arange(half_size, dtype=jnp.float32) * 2.0 / vectors.shape[-1])
    angles = position[..., None] * frequency
    cosine = jnp.cos(angles)
    sine_part = jnp.sin(angles)
    lower_half = vectors[..., :half_size]
    upper_half = vectors[..., half_size:]
    return jnp.concatenate([lower_half * cosine - upper_half * sine_part, upper_half * cosine + lower_half * sine_part], axis=-1)

def block_softmax(scores, valid):
    masked = jnp.where(valid, scores, -1e+30)
    top_score = lax.optimization_barrier(jnp.max(masked, axis=-1))
    weights = jnp.where(valid, jnp.exp(masked - top_score[..., None]), 0.0)
    return (top_score, lax.optimization_barrier(jnp.sum(weights, axis=-1)), weights.astype(jnp.bfloat16))

def reference(hidden_in, norm_gain, q_weight, q_bias, kv_weight, kv_bias, o_weight, q_delta, q_scale_exp, kv_delta, kv_scale_exp, o_delta, o_scale_exp, key_cache, value_cache, cache_lengths):
    fresh_q = refresh(q_weight, q_delta, q_scale_exp)
    fresh_kv = refresh(kv_weight, kv_delta, kv_scale_exp)
    fresh_o = refresh(o_weight, o_delta, o_scale_exp)
    normed = rms_norm(hidden_in, norm_gain).reshape(STEPS * BATCH, D)
    query = jnp.dot(normed, fresh_q.T, preferred_element_type=jnp.float32) + q_bias.astype(jnp.float32)
    keyval = jnp.dot(normed, fresh_kv.reshape(2 * KVW, D).T, preferred_element_type=jnp.float32) + kv_bias.reshape(2 * KVW).astype(jnp.float32)
    position = cache_lengths.astype(jnp.float32)[None, :] + jnp.arange(STEPS, dtype=jnp.float32)[:, None]
    query = rotate(query.reshape(STEPS, BATCH, QH, HD), position[:, :, None]).astype(jnp.bfloat16)
    new_key = rotate(keyval[:, :KVW].reshape(STEPS, BATCH, KVH, HD), position[:, :, None]).astype(jnp.bfloat16)
    new_value = keyval[:, KVW:].reshape(STEPS, BATCH, KVH, HD).astype(jnp.bfloat16)
    group_size = QH // KVH
    half_span = CTX // 2
    inv_root = HD ** (-0.5)
    grouped = query.reshape(STEPS, BATCH, KVH, group_size, HD).astype(jnp.float32)
    cached_keys = key_cache.reshape(BATCH, KVH, 2, half_span, HD).astype(jnp.float32)
    cached_values = value_cache.reshape(BATCH, KVH, 2, half_span, HD).astype(jnp.float32)
    fresh_keys = new_key.astype(jnp.float32)
    fresh_values = new_value.astype(jnp.float32)
    slots = jnp.arange(half_span, dtype=jnp.int32)[None, :]
    limits = cache_lengths.astype(jnp.int32)[:, None]
    low_scores = jnp.einsum('sbgqd,bgpd->sbgqp', grouped, cached_keys[:, :, 0]) * inv_root
    new_scores = jnp.einsum('sbgqd,tbgd->sbgqt', grouped, fresh_keys) * inv_root
    low_valid = jnp.broadcast_to((slots < limits)[None, :, None, None, :], low_scores.shape)
    step_ids = jnp.arange(STEPS, dtype=jnp.int32)
    new_valid = jnp.broadcast_to((step_ids[None, :] <= step_ids[:, None])[:, None, None, None, :], new_scores.shape)
    top_a, total_a, weights_a = block_softmax(jnp.concatenate([low_scores, new_scores], axis=-1), jnp.concatenate([low_valid, new_valid], axis=-1))
    weights_a = weights_a.astype(jnp.float32)
    acc_a = jnp.einsum('sbgqp,bgpd->sbgqd', weights_a[..., :half_span], cached_values[:, :, 0]) + jnp.einsum('sbgqt,tbgd->sbgqd', weights_a[..., half_span:], fresh_values)
    high_scores = jnp.einsum('sbgqd,bgpd->sbgqp', grouped, cached_keys[:, :, 1]) * inv_root
    high_valid = jnp.broadcast_to((slots + half_span < limits)[None, :, None, None, :], high_scores.shape)
    top_b, total_b, weights_b = block_softmax(high_scores, high_valid)
    acc_b = jnp.einsum('sbgqp,bgpd->sbgqd', weights_b.astype(jnp.float32), cached_values[:, :, 1])
    top_all = jnp.maximum(top_a, top_b)
    factor_a = jnp.exp(top_a - top_all)
    factor_b = jnp.exp(top_b - top_all)
    attention = (factor_a[..., None] * acc_a + factor_b[..., None] * acc_b) / (factor_a * total_a + factor_b * total_b)[..., None]
    attention = attention.reshape(STEPS * BATCH, QW).astype(jnp.bfloat16)
    mixed = jnp.dot(attention, fresh_o.T, preferred_element_type=jnp.float32).reshape(STEPS, BATCH, D)
    return (hidden_in.astype(jnp.float32) + mixed).astype(jnp.bfloat16)
```

```python
import functools

import jax
import jax.numpy as jnp
from jax import lax
from jax.experimental import pallas as pl
from jax.experimental.pallas import tpu as pltpu
from jax.sharding import PartitionSpec as P

HD = 128
BLOCK = 32
F32 = jnp.float32
BF16 = jnp.bfloat16
FR = ("fsdp", "rep")
MB = 1 << 20


def swap(x, axis, xor):
    return lax.ppermute(x, axis, [(i, i ^ xor) for i in range(lax.axis_size(axis))])


def nt_dot(a, b):
    return lax.dot_general(a, b, (((1,), (1,)), ((), ())), preferred_element_type=F32)


def params(mib):
    return pltpu.CompilerParams(vmem_limit_bytes=mib * MB)


def expand(exponents, width):
    blocks = exponents.shape[1]
    factor = jnp.exp2(exponents.astype(F32)).astype(BF16)
    row = lax.broadcasted_iota(jnp.int32, (blocks, width), 0)
    col = lax.broadcasted_iota(jnp.int32, (blocks, width), 1)
    spread = jnp.where((col >> 5) == row, 1.0, 0.0).astype(BF16)
    return jnp.dot(factor, spread, preferred_element_type=F32)


def refreshed(base, delta, exponents):
    change = delta.astype(F32) * expand(exponents, delta.shape[1])
    return (base.astype(F32) + change).astype(BF16)


def fresh_qkv_kernel(at, qw, kvw, qd, qe, kvd, kve, first, second):
    half = qw.shape[0] // 2
    query = refreshed(qw[...], qd[...], qe[...])
    first[:half] = query[:half]
    second[:half] = query[half:]
    first[half:] = refreshed(kvw[0], kvd[0], kve[0])
    second[half:] = refreshed(kvw[1], kvd[1], kve[1])


def fresh_qkv(place, q_weight, kv_weight, q_delta, q_exp, kv_delta, kv_exp):
    rows, width = q_delta.shape
    narrow = kv_delta.shape[1]
    if width % 128:
        start = place[0] * width
        q_weight = lax.dynamic_slice_in_dim(q_weight, start, width, 1)
        kv_weight = lax.dynamic_slice_in_dim(kv_weight, start, width, 2)
        place = jnp.zeros_like(place)
    whole = lambda a: pl.BlockSpec(a.shape, lambda i, at: (0,) * a.ndim)
    out = jax.ShapeDtypeStruct((rows // 2 + narrow, width), BF16)
    return pl.pallas_call(
        fresh_qkv_kernel,
        out_shape=(out, out),
        grid_spec=pltpu.PrefetchScalarGridSpec(
            num_scalar_prefetch=1,
            grid=(1,),
            in_specs=[
                pl.BlockSpec((rows, width), lambda i, at: (0, at[0])),
                pl.BlockSpec((2, narrow, width), lambda i, at: (0, 0, at[0])),
                whole(q_delta),
                whole(q_exp),
                whole(kv_delta),
                whole(kv_exp),
            ],
            out_specs=(whole(out), whole(out)),
        ),
        compiler_params=params(16),
        name="fresh_qkv",
    )(place, q_weight, kv_weight, q_delta, q_exp, kv_delta, kv_exp)


def fresh_o_kernel(at, ow, od, oe, *outs):
    rows = outs[0].shape[0]
    for i, out in enumerate(outs):
        part = slice(i * rows, (i + 1) * rows)
        out[...] = refreshed(ow[part], od[part], oe[part])


def fresh_o(place, o_weight, o_delta, o_exp, parts):
    rows, width = o_delta.shape
    whole = lambda a: pl.BlockSpec(a.shape, lambda i, at: (0,) * a.ndim)
    out = jax.ShapeDtypeStruct((rows // parts, width), BF16)
    return pl.pallas_call(
        fresh_o_kernel,
        out_shape=(out,) * parts,
        grid_spec=pltpu.PrefetchScalarGridSpec(
            num_scalar_prefetch=1,
            grid=(1,),
            in_specs=[
                pl.BlockSpec((rows, width), lambda i, at: (at[0], 0)),
                whole(o_delta),
                whole(o_exp),
            ],
            out_specs=(whole(out),) * parts,
        ),
        compiler_params=params(16),
        name="fresh_o",
    )(place, o_weight, o_delta, o_exp)


def norm_kernel(hidden, gain, out):
    values = hidden[0].astype(F32)
    root = lax.rsqrt(jnp.mean(values * values, axis=-1, keepdims=True) + 1e-06)
    out[...] = (values * root * gain[...]).astype(BF16)


def normalize(hidden, gain):
    steps, rows, width = hidden.shape
    tile = min(rows, 64)
    return pl.pallas_call(
        norm_kernel,
        out_shape=jax.ShapeDtypeStruct((steps * rows, width), BF16),
        grid=(steps, rows // tile),
        in_specs=[
            pl.BlockSpec((1, tile, width), lambda s, r: (s, r, 0)),
            pl.BlockSpec((1, width), lambda s, r: (0, 0)),
        ],
        out_specs=pl.BlockSpec((tile, width), lambda s, r: (s * (rows // tile) + r, 0)),
        compiler_params=params(16),
        name="norm",
    )(hidden, gain.reshape(1, width))


def project_kernel(count, at, normed, *refs):
    shards, (out0, out1) = refs[: 2 * count], refs[2 * count :]
    for half, out in enumerate((out0, out1)):
        total = None
        for n in range(count):
            shard = shards[2 * n + half][...]
            width = shard.shape[1]
            cols = pl.ds(pl.multiple_of(at[n] * width, 128), width)
            term = nt_dot(normed[:, cols], shard)
            total = term if total is None else total + term
        out[...] = total


def project(places, normed, shards):
    count = len(shards)
    out = jax.ShapeDtypeStruct((normed.shape[0], shards[0][0].shape[0]), F32)
    vmem = pl.BlockSpec(memory_space=pltpu.VMEM)
    return pl.pallas_call(
        functools.partial(project_kernel, count),
        out_shape=(out, out),
        in_specs=[pl.BlockSpec(memory_space=pltpu.SMEM)] + [vmem] * (1 + 2 * count),
        out_specs=(vmem, vmem),
        compiler_params=params(24),
        name="project",
    )(places, normed, *[a for pair in shards for a in pair])


def finish_kernel(
    count, steps, at, parity, normed, total0, total1, qb, kvb, cosine, sine, *refs
):
    shards, (own, other, packed) = refs[: 2 * count], refs[2 * count :]
    totals = [total0[...], total1[...]]
    for n in range(count):
        width = shards[2 * n].shape[1]
        cols = pl.ds(pl.multiple_of(at[n] * width, 128), width)
        for half in range(2):
            totals[half] = totals[half] + nt_dot(normed[:, cols], shards[2 * n + half][...])
    span = qb.shape[1] // 2
    for half in range(2):
        for head in range(span // HD):
            lanes = slice(head * HD, (head + 1) * HD)
            cols = slice(half * span + head * HD, half * span + (head + 1) * HD)
            query = totals[half][:, lanes] + qb[:, cols].astype(F32)
            turned = query * cosine[...] + pltpu.roll(query, HD // 2, 1) * sine[...]
            packed[:, cols] = turned.astype(BF16)
    key = totals[0][:, span:] + kvb[0:1].astype(F32)
    value = totals[1][:, span:] + kvb[1:2].astype(F32)
    high = key.astype(BF16)
    rest = key - high.astype(F32)
    middle = rest.astype(BF16)
    low = (rest - middle.astype(F32)).astype(BF16)
    packed[:, 2 * span : 2 * span + HD] = jnp.concatenate([high, middle], axis=1)
    packed[:, 2 * span + HD :] = jnp.concatenate([low, value.astype(BF16)], axis=1)
    rows = packed.shape[0] // steps
    near = pl.multiple_of(parity[0] * (rows // 2), 16)
    far = pl.multiple_of((1 - parity[0]) * (rows // 2), 16)
    for s in range(steps):
        own[s] = packed[pl.ds(s * rows + near, rows // 2), :]
        other[s] = packed[pl.ds(s * rows + far, rows // 2), :]


def finish(places, parity, normed, totals, q_bias, kv_bias, cosine, sine, shards, steps):
    count = len(shards)
    rows = normed.shape[0] // steps
    width = q_bias.shape[0] + 2 * HD
    vmem = pl.BlockSpec(memory_space=pltpu.VMEM)
    smem = pl.BlockSpec(memory_space=pltpu.SMEM)
    out = jax.ShapeDtypeStruct((steps, rows // 2, width), BF16)
    return pl.pallas_call(
        functools.partial(finish_kernel, count, steps),
        out_shape=(out, out),
        in_specs=[smem, smem] + [vmem] * (7 + 2 * count),
        out_specs=(vmem, vmem),
        scratch_shapes=[pltpu.VMEM((steps * rows, width), BF16)],
        compiler_params=params(24),
        name="finish",
    )(
        places, parity, normed, *totals, q_bias.reshape(1, -1), kv_bias, cosine, sine,
        *[a for pair in shards for a in pair],
    )


GROUP = 16


def attend_kernel(
    parity, own, other, cosine, sine, keys, values, swapped, near_ok, far_ok, out, new_k, new_v
):
    steps, rows, width = own.shape
    heads = (width - 2 * HD) // HD
    half = HD // 2
    even = parity[0] == 0
    scale = HD ** (-0.5)
    base = width - 2 * HD

    def key_of(ref, s):
        top = ref[s, :, base : base + HD].astype(F32)
        rest = ref[s, :, base + HD :].astype(F32)
        return top[:, :half] + (top[:, half:] + rest[:, :half]), rest[:, half:]

    for s in range(steps):
        key_a, value_a = key_of(own, s)
        key_b, value_b = key_of(other, s)
        key = jnp.where(
            even,
            jnp.concatenate([key_a, key_b], axis=1),
            jnp.concatenate([key_b, key_a], axis=1),
        )
        value = jnp.where(
            even,
            jnp.concatenate([value_a, value_b], axis=1),
            jnp.concatenate([value_b, value_a], axis=1),
        )
        at = pl.ds(pl.multiple_of(s * 2 * rows + parity[0] * rows, 16), rows)
        turned = key * cosine[at, :] + pltpu.roll(key, half, 1) * sine[at, :]
        new_k[s] = turned.astype(BF16)
        new_v[s] = value.astype(BF16)

    span = keys.shape[1]
    count = steps * 2 * heads * GROUP
    lane = GROUP * span
    row_of = lax.broadcasted_iota(jnp.int32, (count, lane), 0) & (GROUP - 1)
    diagonal = row_of == lax.broadcasted_iota(jnp.int32, (count, lane), 1) // span
    fresh = GROUP * steps
    fresh_row = lax.broadcasted_iota(jnp.int32, (count, fresh), 0)
    fresh_col = lax.broadcasted_iota(jnp.int32, (count, fresh), 1)
    fresh_ok = jnp.logical_and(
        (fresh_row & (GROUP - 1)) == (fresh_col & (GROUP - 1)),
        fresh_col // GROUP <= fresh_row // (2 * heads * GROUP),
    )
    lowest = -1e30
    for g in range(rows // GROUP):
        at = slice(g * GROUP, (g + 1) * GROUP)
        query = jnp.concatenate(
            [
                ref[s, at, h * HD : (h + 1) * HD]
                for s in range(steps)
                for ref in (own, other)
                for h in range(heads)
            ],
            axis=0,
        )
        near_k = keys[at].reshape(lane, HD)
        near_v = values[at].reshape(lane, HD)
        far_k = swapped[0, at].reshape(lane, HD)
        far_v = swapped[1, at].reshape(lane, HD)
        fresh_k = jnp.concatenate([new_k[s, at] for s in range(steps)], axis=0)
        fresh_v = jnp.concatenate([new_v[s, at] for s in range(steps)], axis=0)
        ok_n = jnp.logical_and(diagonal, near_ok[g : g + 1, :] > 0)
        ok_f = jnp.logical_and(diagonal, far_ok[g : g + 1, :] > 0)
        score_n = jnp.where(ok_n, nt_dot(query, near_k) * scale, lowest)
        score_f = jnp.where(ok_f, nt_dot(query, far_k) * scale, lowest)
        score_x = jnp.where(fresh_ok, nt_dot(query, fresh_k) * scale, lowest)
        top_n = jnp.max(score_n, axis=1, keepdims=True)
        top_f = jnp.max(score_f, axis=1, keepdims=True)
        top_x = jnp.max(score_x, axis=1, keepdims=True)
        top_n = jnp.where(even, jnp.maximum(top_n, top_x), top_n)
        top_f = jnp.where(even, top_f, jnp.maximum(top_f, top_x))
        top_x = jnp.where(even, top_n, top_f)
        weight_n = jnp.where(ok_n, jnp.exp(score_n - top_n), 0.0)
        weight_f = jnp.where(ok_f, jnp.exp(score_f - top_f), 0.0)
        weight_x = jnp.where(fresh_ok, jnp.exp(score_x - top_x), 0.0)
        top_all = jnp.maximum(top_n, top_f)
        factor_n = jnp.exp(top_n - top_all)
        factor_f = jnp.exp(top_f - top_all)
        factor_x = jnp.where(even, factor_n, factor_f)
        acc = (
            factor_n * jnp.dot(weight_n.astype(BF16), near_v, preferred_element_type=F32)
            + factor_f * jnp.dot(weight_f.astype(BF16), far_v, preferred_element_type=F32)
            + factor_x * jnp.dot(weight_x.astype(BF16), fresh_v, preferred_element_type=F32)
        )
        total = (
            factor_n * jnp.sum(weight_n, axis=1, keepdims=True)
            + factor_f * jnp.sum(weight_f, axis=1, keepdims=True)
            + factor_x * jnp.sum(weight_x, axis=1, keepdims=True)
        )
        result = (acc / total).astype(BF16)
        for s in range(steps):
            for h in range(2 * heads):
                first = (s * 2 * heads + h) * GROUP
                out[s, at, h * HD : (h + 1) * HD] = result[first : first + GROUP]


def attend(parity, own, other, cosine, sine, keys, values, swapped, near_ok, far_ok):
    steps, rows, width = own.shape
    span = keys.shape[1]
    whole = lambda a: pl.BlockSpec(a.shape, lambda i, at: (0,) * a.ndim)
    half = pl.BlockSpec((rows, span, HD), lambda i, at: (at[0], 0, 0))
    out = jax.ShapeDtypeStruct((steps, rows, 2 * (width - 2 * HD)), BF16)
    return pl.pallas_call(
        attend_kernel,
        out_shape=out,
        grid_spec=pltpu.PrefetchScalarGridSpec(
            num_scalar_prefetch=1,
            grid=(1,),
            in_specs=[
                whole(own), whole(other), whole(cosine), whole(sine), half, half,
                whole(swapped), whole(near_ok), whole(far_ok),
            ],
            out_specs=whole(out),
            scratch_shapes=[pltpu.VMEM((steps, rows, HD), BF16)] * 2,
        ),
        compiler_params=params(24),
        name="attend",
    )(parity, own, other, cosine, sine, keys, values, swapped, near_ok, far_ok)


def pick_kernel(at, *refs):
    count = len(refs) // 2
    for k in range(count):
        for i in range(count):

            @pl.when((at[0] ^ k) == i)
            def _(k=k, i=i):
                refs[count + k][...] = refs[i][...]


def pick(where, blocks):
    vmem = pl.BlockSpec(memory_space=pltpu.VMEM)
    return pl.pallas_call(
        pick_kernel,
        out_shape=tuple(jax.ShapeDtypeStruct(b.shape, b.dtype) for b in blocks),
        in_specs=[pl.BlockSpec(memory_space=pltpu.SMEM)] + [vmem] * len(blocks),
        out_specs=(vmem,) * len(blocks),
        compiler_params=params(8),
        name="pick",
    )(where, *blocks)


def output_kernel(count, at, parity, a0, a1, a2, a3, hidden, *refs):
    shards, out, weight = refs[:count], refs[count], refs[count + 1]
    rows = shards[0].shape[0] // 4
    width = shards[0].shape[1]
    for n, shard in enumerate(shards):
        place = pl.ds(pl.multiple_of(at[n] * rows, 16), rows)
        for k in range(4):
            weight[place, k * width : (k + 1) * width] = shard[k * rows : (k + 1) * rows]
    steps, half = a0.shape[:2]
    near = pl.multiple_of(parity[0] * half, 16)
    far = pl.multiple_of((1 - parity[0]) * half, 16)
    flat = lambda ref: ref[...].reshape(steps * half, 2 * width)
    b1, b3 = flat(a1), flat(a3)
    top = nt_dot(flat(a0), weight[:, : 2 * width]) + nt_dot(flat(a2), weight[:, 2 * width :])
    low = (
        nt_dot(b1[:, :width], weight[:, width : 2 * width])
        + nt_dot(b1[:, width:], weight[:, :width])
        + nt_dot(b3[:, :width], weight[:, 3 * width :])
        + nt_dot(b3[:, width:], weight[:, 2 * width : 3 * width])
    )
    for start, total in ((near, top), (far, low)):
        for s in range(steps):
            place = pl.ds(start, half)
            mixed = total[s * half : (s + 1) * half]
            out[s, place, :] = (hidden[s, place, :].astype(F32) + mixed).astype(BF16)


def output(places, parity, column, parts, hidden, shards):
    steps, half, _ = parts[0].shape
    rows = hidden.shape[1]
    width = shards[0].shape[0] // 4 * len(shards)
    depth = shards[0].shape[1]
    whole = lambda a: pl.BlockSpec(a.shape, lambda i, *at: (0,) * a.ndim)
    out = jax.ShapeDtypeStruct((steps, rows, width), BF16)
    return pl.pallas_call(
        lambda at, parity, column, *refs: output_kernel(len(shards), at, parity, *refs),
        out_shape=out,
        grid_spec=pltpu.PrefetchScalarGridSpec(
            num_scalar_prefetch=3,
            grid=(1,),
            in_specs=[whole(p) for p in parts]
            + [pl.BlockSpec((steps, rows, width), lambda i, at, p, c: (0, 0, c[0]))]
            + [whole(s) for s in shards],
            out_specs=whole(out),
            scratch_shapes=[pltpu.VMEM((width, 4 * depth), BF16)],
        ),
        compiler_params=params(32),
        name="output",
    )(places, parity, column, *parts, hidden, *shards)


def one(value):
    return jnp.asarray(value, jnp.int32).reshape(1)


def shards(
    hidden_in,
    norm_gain,
    q_weight,
    q_bias,
    kv_weight,
    kv_bias,
    o_weight,
    q_delta,
    q_scale_exp,
    kv_delta,
    kv_scale_exp,
    o_delta,
    o_scale_exp,
    key_cache,
    value_cache,
    cache_lengths,
):
    steps, rows, model_width = hidden_in.shape
    q_width = q_weight.shape[0]
    span = key_cache.shape[2]
    half = rows // 2
    fsdp, tp, rep = (lax.axis_size(a) for a in ("fsdp", "tp", "rep"))
    f, t, r = (lax.axis_index(a) for a in ("fsdp", "tp", "rep"))
    shard_width = q_delta.shape[1]
    col_width = model_width // tp
    small = fsdp == 4 and tp == 4 and rep == 2 and shard_width % 128 == 0 and col_width % 128 == 0
    parity = t % 2
    parity_ref = one(parity)
    place = one(f * rep + r)

    far_start = (1 - parity) * half
    far_cache = jnp.stack(
        [lax.dynamic_slice_in_dim(c[:, 0], far_start, half, 0) for c in (key_cache, value_cache)]
    )
    swapped = swap(far_cache, "tp", 1)

    first, second = fresh_qkv(
        place, q_weight, kv_weight, q_delta, q_scale_exp, kv_delta, kv_scale_exp
    )
    normed = normalize(hidden_in, norm_gain)

    position = (
        cache_lengths.astype(F32)[None, :] + jnp.arange(steps, dtype=F32)[:, None]
    ).reshape(-1, 1)
    frequency = 1000000.0 ** (-jnp.arange(HD // 2, dtype=F32) * 2.0 / HD)
    angles = position * frequency
    cosine, sine = jnp.cos(angles), jnp.sin(angles)
    cosine = jnp.concatenate([cosine, cosine], axis=1)
    sine = jnp.concatenate([-sine, sine], axis=1)

    own_lengths = lax.dynamic_slice_in_dim(cache_lengths, parity * half, half, 0)
    slot = jnp.arange(span, dtype=jnp.int32)[None, :]
    near_ok = (slot + parity * span < own_lengths[:, None]).astype(jnp.int32)
    far_ok = (slot + (1 - parity) * span < own_lengths[:, None]).astype(jnp.int32)
    near_ok = near_ok.reshape(half // GROUP, GROUP * span)
    far_ok = far_ok.reshape(half // GROUP, GROUP * span)

    if small:
        o_parts = fresh_o(place, o_weight, o_delta, o_scale_exp, 4)
        x1, y2 = swap(first, "fsdp", 1), swap(second, "fsdp", 2)
        x2, y1 = swap(second, "fsdp", 1), swap(first, "fsdp", 2)
        d1, d2 = swap(x1, "fsdp", 2), swap(y2, "fsdp", 1)
        near = [(first, second), (x1, x2), (y1, y2)]
        across = [tuple(swap(a, "rep", 1) for a in pair) for pair in near]
        last = [(d1, d2), (swap(d1, "rep", 1), swap(d2, "rep", 1))]
        at = lambda i, j: (f ^ i) * rep + (r ^ j)
        early_at = jnp.stack([at(i, j) for j in (0, 1) for i in (0, 1, 2)]).astype(jnp.int32)
        last_at = jnp.stack([at(3, 0), at(3, 1)]).astype(jnp.int32)
        totals = project(early_at, normed, near + across)
        own, other = finish(
            last_at, parity_ref, normed, totals, q_bias, kv_bias, cosine, sine, last, steps
        )
    else:
        full = [lax.all_gather(a, FR, axis=1, tiled=True) for a in (first, second)]
        totals = [jnp.dot(normed, a.T, preferred_element_type=F32) for a in full]
        own, other = finish(
            place, parity_ref, normed, totals, q_bias, kv_bias, cosine, sine, [], steps
        )

    received = swap(other, "tp", 1)
    attention = attend(
        parity_ref, own, received, cosine, sine, key_cache[:, 0], value_cache[:, 0], swapped,
        near_ok, far_ok,
    )

    if small:
        quarters = [o_parts[0]] + [swap(o_parts[i], "fsdp", i) for i in (1, 2, 3)]
        picked = pick(one(f ^ t), quarters)
        blocks = [picked[0]] + [swap(picked[k], "tp", k) for k in (1, 2, 3)]
        stacked = jnp.concatenate(blocks, axis=0)
        o_near = [stacked] + [swap(stacked, "fsdp", i) for i in (1, 2, 3)]
        o_far = [swap(a, "rep", 1) for a in o_near]
        spot = lambda i, j: (r ^ j) * 4 + (f ^ i ^ t)
        o_at = jnp.stack([spot(i, j) for j in (0, 1) for i in range(4)]).astype(jnp.int32)
        parts = [attention] + [swap(attention, "tp", k) for k in (1, 2, 3)]
        return output(o_at, parity_ref, one(t), parts, hidden_in, o_near + o_far)

    own_o = fresh_o(place, o_weight, o_delta, o_scale_exp, 1)[0]
    full_o = lax.all_gather(own_o, FR, axis=0, tiled=True)
    own_cols = lax.all_to_all(
        full_o.reshape(tp, col_width, q_width), "tp", split_axis=0, concat_axis=2, tiled=True
    ).reshape(col_width, tp * q_width)
    everyone = lax.all_gather(attention, "tp", axis=0)
    everyone = everyone.reshape(tp // 2, 2, steps, half, 2, q_width)
    odd = everyone[:, 1][:, :, :, ::-1]
    everyone = jnp.stack([everyone[:, 0], odd], axis=0)
    features = everyone.transpose(2, 0, 3, 1, 4, 5).reshape(steps * rows, tp * q_width)
    mixed = jnp.dot(features, own_cols.T, preferred_element_type=F32)
    residual = lax.dynamic_slice_in_dim(hidden_in, t * col_width, col_width, 2).astype(F32)
    return (residual + mixed.reshape(steps, rows, col_width)).astype(BF16)


def solution(mesh):
    placed = (
        P(None, ("fsdp", "rep"), None),
        P(),
        P("tp", None),
        P("tp"),
        P(None, "tp", None),
        P(None, "tp"),
        P(None, "tp"),
        P("tp", ("fsdp", "rep")),
        P("tp", ("fsdp", "rep")),
        P(None, "tp", ("fsdp", "rep")),
        P(None, "tp", ("fsdp", "rep")),
        P(("fsdp", "rep"), "tp"),
        P(("fsdp", "rep"), "tp"),
        P(("fsdp", "rep"), "tp", None, None),
        P(("fsdp", "rep"), "tp", None, None),
        P(("fsdp", "rep")),
    )
    return jax.shard_map(
        shards,
        mesh=mesh,
        in_specs=placed,
        out_specs=P(None, ("fsdp", "rep"), "tp"),
        check_vma=False,
    )
```

```python
import functools
import math

import jax
import jax.numpy as jnp
from jax import lax
from jax.experimental import pallas as pl
from jax.experimental.pallas import tpu as pltpu
from jax.sharding import PartitionSpec as P

HD = 128
BLOCK = 32
F32 = jnp.float32
BEGIN_MIB = 61.8
BF16 = jnp.bfloat16
FR = ("fsdp", "rep")
MB = 1 << 20


def swap(x, axis, xor):
    return lax.ppermute(x, axis, [(i, i ^ xor) for i in range(lax.axis_size(axis))])


def nt_dot(a, b):
    return lax.dot_general(a, b, (((1,), (1,)), ((), ())), preferred_element_type=F32)


def call(kernel, name, mib, weight=1024, **kw):
    return pl.pallas_call(
        kernel,
        compiler_params=pltpu.CompilerParams(vmem_limit_bytes=int(mib * MB)),
        cost_estimate=pl.CostEstimate(flops=1024, bytes_accessed=weight, transcendentals=0),
        name=name,
        **kw,
    )


def sds(shape, dtype):
    return jax.ShapeDtypeStruct(shape, dtype)


HBM = pl.BlockSpec(memory_space=pltpu.HBM)
VMEM = pl.BlockSpec(memory_space=pltpu.VMEM)
ANY = pl.BlockSpec(memory_space=pl.ANY)
DMA = pltpu.SemaphoreType.DMA


def shard_index():
    return lax.axis_index("fsdp") * lax.axis_size("rep") + lax.axis_index("rep")


def half_rows(which, half):
    return pl.multiple_of(((lax.axis_index("tp") % 2) ^ which) * half, 16)


def refreshed(base, delta, exponents):
    blocks, width = exponents.shape[0], delta.shape[1]
    factor = jnp.exp2(exponents.astype(F32)).astype(BF16)
    row = lax.broadcasted_iota(jnp.int32, (blocks, width), 0)
    col = lax.broadcasted_iota(jnp.int32, (blocks, width), 1)
    spread = jnp.where((col >> 5) == row, 1.0, 0.0).astype(BF16)
    scale = lax.dot_general(factor, spread, (((0,), (0,)), ((), ())), preferred_element_type=F32)
    return (base.astype(F32) + delta.astype(F32) * scale).astype(BF16)


def begin_kernel(
    sliced, parts, qw, kvw, ow, qd, kvd, od, kc, vc, qe, kve, oe, fresh, far, *refs
):
    outs, (qw_v, kvw_v, ow_v, qd_v, kvd_v, od_v, sem) = refs[:parts], refs[parts:]
    rows, width = qd.shape
    cols = pl.ds(0 if sliced else pl.multiple_of(shard_index() * width, 128), width)
    far_rows = pl.ds(half_rows(1, far.shape[1]), far.shape[1])
    o_rows = od.shape[0]
    place = pl.ds(pl.multiple_of(shard_index() * o_rows, 16), o_rows)
    loads = [
        pltpu.make_async_copy(src, dst, sem.at[n])
        for n, (src, dst) in enumerate(
            [
                (qw.at[:, cols], qw_v),
                (qd, qd_v),
                (kvw.at[:, :, cols], kvw_v),
                (kvd, kvd_v),
                (ow.at[place], ow_v),
                (od, od_v),
                (kc.at[far_rows], far.at[0]),
                (vc.at[far_rows], far.at[1]),
            ]
        )
    ]
    for load in loads:
        load.start()
    loads[0].wait()
    loads[1].wait()
    fresh[:rows] = refreshed(qw_v[...], qd_v[...], qe[...])
    loads[2].wait()
    loads[3].wait()
    narrow = kvd.shape[1]
    for n in range(2):
        part = slice(rows + n * narrow, rows + (n + 1) * narrow)
        fresh[part] = refreshed(kvw_v[n], kvd_v[n], kve[:, n, :])
    loads[4].wait()
    loads[5].wait()
    result = refreshed(ow_v[...], od_v[...], oe[...])
    if parts == 1:
        outs[0][...] = result
    else:
        quarter = [result[n * o_rows // 4 : (n + 1) * o_rows // 4] for n in range(4)]
        outs[0][...] = quarter[0]
        outs[1][...] = jnp.concatenate([quarter[1], quarter[3]], axis=0)
        outs[2][...] = quarter[2]
    loads[6].wait()
    loads[7].wait()


def begin(
    parts, q_weight, kv_weight, o_weight, q_delta, q_exp, kv_delta, kv_exp, o_delta, o_exp,
    keys, values,
):
    rows, width = q_delta.shape
    narrow = kv_delta.shape[1]
    sliced = width % 128 != 0
    if sliced:
        start = shard_index() * width
        q_weight = lax.dynamic_slice_in_dim(q_weight, start, width, 1)
        kv_weight = lax.dynamic_slice_in_dim(kv_weight, start, width, 2)
    sizes = (4,) if parts == 1 else (1, 2, 1)
    pair = lambda a: [pltpu.VMEM(a.shape, BF16)]
    return call(
        functools.partial(begin_kernel, sliced, parts),
        "begin",
        BEGIN_MIB,
        out_shape=(
            sds((rows + 2 * narrow, width), BF16),
            sds((2, keys.shape[0] // 2) + keys.shape[1:], BF16),
        )
        + tuple(sds((o_delta.shape[0] * n // 4, o_delta.shape[1]), BF16) for n in sizes),
        in_specs=[HBM] * 8 + [VMEM] * 3,
        out_specs=(VMEM,) * (2 + parts),
        scratch_shapes=(pair(q_delta) + pair(kv_delta) + pair(o_delta)) * 2 + [DMA((8,))],
    )(
        q_weight, kv_weight, o_weight, q_delta, kv_delta, o_delta, keys, values,
        q_exp.T, kv_exp.transpose(2, 0, 1), o_exp.T,
    )


CHUNKS = 8


def prepare_kernel(hidden, gain, lengths, after, normed, cosine, sine, hidden_v, gain_v, sem):
    steps, rows, _ = hidden.shape
    tile = steps * rows // CHUNKS
    per_step = rows // tile
    loads = []
    for n in range(CHUNKS):
        s, at = n // per_step, pl.ds(n % per_step * tile, tile)
        loads.append(pltpu.make_async_copy(hidden.at[s, at], hidden_v.at[n], sem.at[n]))
    loads.append(pltpu.make_async_copy(gain, gain_v, sem.at[CHUNKS]))
    for load in loads:
        load.start()
    lane = lax.broadcasted_iota(jnp.int32, (1, HD), 1) & (HD // 2 - 1)
    frequency = jnp.exp(lane.astype(F32) * (-2.0 / HD * math.log(1000000.0)))
    length = jnp.broadcast_to(lengths[...].astype(F32), (HD, rows)).T
    low = lax.broadcasted_iota(jnp.int32, (1, HD), 1) < HD // 2
    for s in range(steps):
        angles = (length + float(s)) * frequency
        at = slice(s * rows, (s + 1) * rows)
        cosine[at] = jnp.cos(angles)
        turned = jnp.sin(angles)
        sine[at] = jnp.where(low, -turned, turned)
    loads[CHUNKS].wait()
    for n in range(CHUNKS):
        loads[n].wait()
        values = hidden_v[n].astype(F32)
        root = lax.rsqrt(jnp.mean(values * values, axis=-1, keepdims=True) + 1e-06)
        normed[n * tile : (n + 1) * tile] = (values * root * gain_v[...]).astype(BF16)


def prepare(hidden, gain, lengths, after):
    steps, rows, width = hidden.shape
    table = sds((steps * rows, HD), F32)
    return call(
        prepare_kernel,
        "prepare",
        16,
        weight=10 * MB,
        out_shape=(sds((steps * rows, width), BF16), table, table),
        in_specs=[HBM, HBM, VMEM, ANY],
        out_specs=(VMEM,) * 3,
        scratch_shapes=[
            pltpu.VMEM((CHUNKS, steps * rows // CHUNKS, width), BF16),
            pltpu.VMEM((1, width), F32),
            DMA((CHUNKS + 1,)),
        ],
    )(hidden, gain.reshape(1, width), lengths.reshape(1, rows), after)


def halves_kernel(along_x, along_y, *refs):
    first, second, both = refs[-3:]
    rows = along_x.shape[0]
    first[...] = along_x[: rows // 2]
    second[...] = along_y[rows // 2 :]
    both[:rows] = along_x[...]
    both[rows:] = along_y[...]


def halves(along_x, along_y, after):
    rows, width = along_x.shape
    out = sds((rows // 2, width), BF16)
    return call(
        halves_kernel,
        "halves",
        8,
        out_shape=(out, out, sds((2 * rows, width), BF16)),
        in_specs=[VMEM, VMEM] + [ANY] * len(after),
        out_specs=(VMEM,) * 3,
    )(along_x, along_y, *after)


def term(place, normed, shard):
    width = shard.shape[1]
    owner = (lax.axis_index("fsdp") ^ place[0]) * lax.axis_size("rep")
    owner += lax.axis_index("rep") ^ place[1]
    return nt_dot(normed[:, pl.ds(pl.multiple_of(owner * width, 128), width)], shard)


def project_kernel(places, rows, normed, *refs):
    total = None
    for group, ref in zip(places, refs):
        for n, place in enumerate(group):
            part = term(place, normed, ref[n * rows : (n + 1) * rows])
            total = part if total is None else total + part
    refs[-1][...] = total


def project(places, normed, shards):
    rows = shards[0].shape[0]
    return call(
        functools.partial(project_kernel, places, rows),
        "project",
        16,
        out_shape=sds((normed.shape[0], rows), F32),
        in_specs=[VMEM] * (1 + len(shards)),
        out_specs=VMEM,
    )(normed, *shards)


def finish_kernel(places, steps, normed, total_in, qb, kvb, cosine, sine, *refs):
    own, other, packed = refs[-3:]
    total = total_in[...]
    for n, place in enumerate(places):
        shard = jnp.concatenate([refs[2 * n][...], refs[2 * n + 1][...]], axis=0)
        total += term(place, normed, shard)
    span = qb.shape[1]
    for head in range(span // HD):
        cols = slice(head * HD, (head + 1) * HD)
        query = total[:, cols] + qb[:, cols].astype(F32)
        turned = query * cosine[...] + pltpu.roll(query, HD // 2, 1) * sine[...]
        packed[:, cols] = turned.astype(BF16)
    key = total[:, span : span + HD // 2] + kvb[0:1].astype(F32)
    value = total[:, span + HD // 2 :] + kvb[1:2].astype(F32)
    high = key.astype(BF16)
    rest = key - high.astype(F32)
    middle = rest.astype(BF16)
    low = (rest - middle.astype(F32)).astype(BF16)
    packed[:, span : span + HD] = jnp.concatenate([high, middle], axis=1)
    packed[:, span + HD :] = jnp.concatenate([low, value.astype(BF16)], axis=1)
    rows = packed.shape[0] // steps
    for s in range(steps):
        own[s] = packed[pl.ds(s * rows + half_rows(0, rows // 2), rows // 2), :]
        other[s] = packed[pl.ds(s * rows + half_rows(1, rows // 2), rows // 2), :]


def finish(places, steps, normed, total, q_bias, kv_bias, cosine, sine, shards):
    rows = normed.shape[0] // steps
    width = q_bias.shape[0] + 2 * HD
    out = sds((steps, rows // 2, width), BF16)
    return call(
        functools.partial(finish_kernel, places, steps),
        "finish",
        16,
        out_shape=(out, out),
        in_specs=[VMEM] * (6 + len(shards)),
        out_specs=(VMEM, VMEM),
        scratch_shapes=[pltpu.VMEM((steps * rows, width), BF16)],
    )(normed, total, q_bias.reshape(1, -1), kv_bias, cosine, sine, *shards)


GROUP = 16


def attend_kernel(
    own, other, cosine, sine, swapped, lengths, keys, values,
    out, new_k, new_v, near_kv, limits, sem
):
    steps, rows, width = own.shape
    heads = (width - 2 * HD) // HD
    half = HD // 2
    parity = lax.axis_index("tp") % 2
    even = parity == 0
    first = half_rows(0, rows)
    loads = [
        pltpu.make_async_copy(src.at[pl.ds(first, rows)], near_kv.at[n], sem.at[n])
        for n, src in enumerate((keys, values))
    ]
    for load in loads:
        load.start()
    limits[...] = jnp.broadcast_to(lengths[...], (HD, lengths.shape[1])).T
    scale = HD ** (-0.5)
    base = width - 2 * HD

    def key_of(ref, s):
        top = ref[s, :, base : base + HD].astype(F32)
        rest = ref[s, :, base + HD :].astype(F32)
        return top[:, :half] + (top[:, half:] + rest[:, :half]), rest[:, half:]

    for s in range(steps):
        key_a, value_a = key_of(own, s)
        key_b, value_b = key_of(other, s)
        key = jnp.where(
            even,
            jnp.concatenate([key_a, key_b], axis=1),
            jnp.concatenate([key_b, key_a], axis=1),
        )
        value = jnp.where(
            even,
            jnp.concatenate([value_a, value_b], axis=1),
            jnp.concatenate([value_b, value_a], axis=1),
        )
        at = pl.ds(pl.multiple_of(s * 2 * rows + first, 16), rows)
        turned = key * cosine[at, :] + pltpu.roll(key, half, 1) * sine[at, :]
        new_k[s] = turned.astype(BF16)
        new_v[s] = value.astype(BF16)

    span = keys.shape[1]
    count = steps * 2 * heads * GROUP
    lane = GROUP * span
    row_of = lax.broadcasted_iota(jnp.int32, (count, lane), 0) & (GROUP - 1)
    column = lax.broadcasted_iota(jnp.int32, (count, lane), 1)
    diagonal = row_of == column // span
    slot = column % span
    fresh = GROUP * steps
    fresh_row = lax.broadcasted_iota(jnp.int32, (count, fresh), 0)
    fresh_col = lax.broadcasted_iota(jnp.int32, (count, fresh), 1)
    fresh_ok = jnp.logical_and(
        (fresh_row & (GROUP - 1)) == (fresh_col & (GROUP - 1)),
        fresh_col // GROUP <= fresh_row // (2 * heads * GROUP),
    )
    lowest = -1e30
    for load in loads:
        load.wait()
    for g in range(rows // GROUP):
        at = slice(g * GROUP, (g + 1) * GROUP)
        query = jnp.concatenate(
            [
                ref[s, at, h * HD : (h + 1) * HD]
                for s in range(steps)
                for ref in (own, other)
                for h in range(heads)
            ],
            axis=0,
        )
        near_k = near_kv[0, at].reshape(lane, HD)
        near_v = near_kv[1, at].reshape(lane, HD)
        far_k = swapped[0, at].reshape(lane, HD)
        far_v = swapped[1, at].reshape(lane, HD)
        fresh_k = jnp.concatenate([new_k[s, at] for s in range(steps)], axis=0)
        fresh_v = jnp.concatenate([new_v[s, at] for s in range(steps)], axis=0)
        limit = limits[pl.ds(first + g * GROUP, GROUP), :1]
        limit = jnp.concatenate([limit] * (count // GROUP), axis=0)
        ok_n = jnp.logical_and(diagonal, slot + parity * span < limit)
        ok_f = jnp.logical_and(diagonal, slot + (1 - parity) * span < limit)
        score_n = jnp.where(ok_n, nt_dot(query, near_k) * scale, lowest)
        score_f = jnp.where(ok_f, nt_dot(query, far_k) * scale, lowest)
        score_x = jnp.where(fresh_ok, nt_dot(query, fresh_k) * scale, lowest)
        top_n = jnp.max(score_n, axis=1, keepdims=True)
        top_f = jnp.max(score_f, axis=1, keepdims=True)
        top_x = jnp.max(score_x, axis=1, keepdims=True)
        top_n = jnp.where(even, jnp.maximum(top_n, top_x), top_n)
        top_f = jnp.where(even, top_f, jnp.maximum(top_f, top_x))
        top_x = jnp.where(even, top_n, top_f)
        weight_n = jnp.where(ok_n, jnp.exp(score_n - top_n), 0.0)
        weight_f = jnp.where(ok_f, jnp.exp(score_f - top_f), 0.0)
        weight_x = jnp.where(fresh_ok, jnp.exp(score_x - top_x), 0.0)
        top_all = jnp.maximum(top_n, top_f)
        factor_n = jnp.exp(top_n - top_all)
        factor_f = jnp.exp(top_f - top_all)
        factor_x = jnp.where(even, factor_n, factor_f)
        acc = (
            factor_n * jnp.dot(weight_n.astype(BF16), near_v, preferred_element_type=F32)
            + factor_f * jnp.dot(weight_f.astype(BF16), far_v, preferred_element_type=F32)
            + factor_x * jnp.dot(weight_x.astype(BF16), fresh_v, preferred_element_type=F32)
        )
        total = (
            factor_n * jnp.sum(weight_n, axis=1, keepdims=True)
            + factor_f * jnp.sum(weight_f, axis=1, keepdims=True)
            + factor_x * jnp.sum(weight_x, axis=1, keepdims=True)
        )
        result = (acc / total).astype(BF16)
        for s in range(steps):
            for h in range(2 * heads):
                place = (s * 2 * heads + h) * GROUP
                out[s, at, h * HD : (h + 1) * HD] = result[place : place + GROUP]


def attend(own, other, cosine, sine, swapped, lengths, keys, values):
    steps, rows, width = own.shape
    return call(
        attend_kernel,
        "attend",
        24,
        out_shape=sds((steps, rows, 2 * (width - 2 * HD)), BF16),
        in_specs=[VMEM] * 6 + [HBM] * 2,
        out_specs=VMEM,
        scratch_shapes=[
            pltpu.VMEM((steps, rows, HD), BF16),
            pltpu.VMEM((steps, rows, HD), BF16),
            pltpu.VMEM((2, rows) + keys.shape[1:], BF16),
            pltpu.VMEM((lengths.shape[0], HD), jnp.int32),
            DMA((2,)),
        ],
    )(own, other, cosine, sine, swapped, lengths.reshape(1, -1), keys, values)


def relay_kernel(own, along_x, after, out):
    rows = own.shape[0]
    out[:rows] = own[...]
    out[rows:] = along_x[rows:]


def relay(own, along_x, after):
    return call(
        relay_kernel,
        "relay",
        8,
        out_shape=sds(along_x.shape, BF16),
        in_specs=[VMEM] * 2 + [ANY],
        out_specs=VMEM,
    )(own, along_x, after)


def pick_kernel(own, along_x, along_y, *refs):
    outs, rows = refs[-4:], own.shape[0]
    blocks = [own[...], along_x[:rows], along_y[:rows], along_y[rows:]]
    where = lax.axis_index("fsdp") ^ lax.axis_index("tp")
    for k, out in enumerate(outs):
        for i, block in enumerate(blocks):

            @pl.when((where ^ k) == i)
            def _(out=out, block=block):
                out[...] = block


def pick(own, along_x, along_y, after):
    return call(
        pick_kernel,
        "pick",
        8,
        out_shape=(sds(own.shape, BF16),) * 4,
        in_specs=[VMEM] * 3 + [ANY] * len(after),
        out_specs=(VMEM,) * 4,
    )(own, along_x, along_y, *after)


def stack_kernel(*refs):
    rows = refs[0].shape[0]
    for n, ref in enumerate(refs[: refs[-1].shape[0] // rows]):
        refs[-1][n * rows : (n + 1) * rows] = ref[...]


def stack(blocks, after):
    rows, width = blocks[0].shape
    return call(
        stack_kernel,
        "stack",
        8,
        out_shape=sds((len(blocks) * rows, width), BF16),
        in_specs=[VMEM] * len(blocks) + [ANY] * len(after),
        out_specs=VMEM,
    )(*blocks, *after)


def assemble_kernel(*refs):
    weight = refs[-1]
    rows, width = refs[0].shape[0] // 4, refs[0].shape[1]
    for j in range(2):
        for i in range(4):
            shard, first = refs[2 * j + min(i, 1)], max(i - 1, 0) * 4
            quarter = lax.axis_index("fsdp") ^ i ^ lax.axis_index("tp")
            place = ((lax.axis_index("rep") ^ j) * 4 + quarter) * rows
            for k in range(4):
                weight[pl.ds(pl.multiple_of(place, 16), rows), k * width : (k + 1) * width] = (
                    shard[(first + k) * rows : (first + k + 1) * rows]
                )


def assemble(*shards):
    rows, width = shards[0].shape
    return call(
        assemble_kernel,
        "assemble",
        16,
        out_shape=sds((2 * rows, 4 * width), BF16),
        in_specs=[VMEM] * len(shards),
        out_specs=VMEM,
    )(*shards)


def output_kernel(weight, a0, a1, a2, a3, hidden, out, hidden_v, sem):
    width = weight.shape[1] // 4
    steps, half = a0.shape[:2]
    cols = out.shape[2]
    place = pl.ds(pl.multiple_of(lax.axis_index("tp") * cols, 128), cols)
    load = pltpu.make_async_copy(hidden.at[:, :, place], hidden_v, sem)
    load.start()
    flat = lambda ref: ref[...].reshape(steps * half, 2 * width)
    b1, b3 = flat(a1), flat(a3)
    top = nt_dot(flat(a0), weight[:, : 2 * width]) + nt_dot(flat(a2), weight[:, 2 * width :])
    low = (
        nt_dot(b1[:, :width], weight[:, width : 2 * width])
        + nt_dot(b1[:, width:], weight[:, :width])
        + nt_dot(b3[:, :width], weight[:, 3 * width :])
        + nt_dot(b3[:, width:], weight[:, 2 * width : 3 * width])
    )
    load.wait()
    for which, total in ((0, top), (1, low)):
        for s in range(steps):
            at = pl.ds(half_rows(which, half), half)
            mixed = total[s * half : (s + 1) * half]
            out[s, at, :] = (hidden_v[s, at, :].astype(F32) + mixed).astype(BF16)


def output(weight, parts, hidden):
    steps, rows, _ = hidden.shape
    shape = (steps, rows, weight.shape[0])
    return call(
        output_kernel,
        "output",
        24,
        out_shape=sds(shape, BF16),
        in_specs=[VMEM] * (1 + len(parts)) + [HBM],
        out_specs=VMEM,
        scratch_shapes=[pltpu.VMEM(shape, BF16), DMA],
    )(weight, *parts, hidden)


def shards(
    hidden_in,
    norm_gain,
    q_weight,
    q_bias,
    kv_weight,
    kv_bias,
    o_weight,
    q_delta,
    q_scale_exp,
    kv_delta,
    kv_scale_exp,
    o_delta,
    o_scale_exp,
    key_cache,
    value_cache,
    cache_lengths,
):
    steps, rows, model_width = hidden_in.shape
    q_width = q_weight.shape[0]
    half = rows // 2
    fsdp, tp, rep = (lax.axis_size(a) for a in ("fsdp", "tp", "rep"))
    shard_width = q_delta.shape[1]
    col_width = model_width // tp
    small = fsdp == 4 and tp == 4 and rep == 2 and shard_width % 128 == 0 and col_width % 128 == 0
    keys, values = key_cache[:, 0], value_cache[:, 0]

    fresh, far, *o_parts = begin(
        3 if small else 1, q_weight, kv_weight, o_weight, q_delta, q_scale_exp, kv_delta,
        kv_scale_exp, o_delta, o_scale_exp, keys, values,
    )
    swapped = swap(far, "tp", 1)
    normed, cosine, sine = prepare(hidden_in, norm_gain, cache_lengths, o_parts[0])

    if small:
        along_x, along_y = swap(fresh, "fsdp", 1), swap(fresh, "fsdp", 2)
        o_x = swap(o_parts[1], "fsdp", 1)
        first, second, both = halves(along_x, along_y, [cosine, o_x])
        last = [swap(first, "fsdp", 2), swap(second, "fsdp", 1)]
        o_parts = [o_parts[0], o_x, swap(relay(o_parts[2], o_x, first), "fsdp", 2)]
        near = [fresh, both]
        near += [swap(a, "rep", 1) for a in near]
        last += [swap(a, "rep", 1) for a in last]
        places = [[(0, 0)], [(1, 0), (2, 0)], [(0, 1)], [(1, 1), (2, 1)]]
        total = project(places, normed, near)
        own, other = finish(
            [(3, 0), (3, 1)], steps, normed, total, q_bias, kv_bias, cosine, sine, last
        )
    else:
        full = lax.all_gather(fresh, FR, axis=1, tiled=True)
        total = jnp.dot(normed, full.T, preferred_element_type=F32)
        own, other = finish([], steps, normed, total, q_bias, kv_bias, cosine, sine, [])

    received = swap(other, "tp", 1)
    attention = attend(own, received, cosine, sine, swapped, cache_lengths, keys, values)

    if small:
        picked = pick(*o_parts, [swapped])
        o_parts = [picked[0]] + [swap(picked[k], "tp", k) for k in (1, 2, 3)]
        parts = [attention] + [swap(attention, "tp", k) for k in (1, 2, 3)]
        stacked = stack(o_parts, [attention])
        others = stack([swap(stacked, "fsdp", i) for i in (1, 2, 3)], parts[1:])
        weight = assemble(stacked, others, swap(stacked, "rep", 1), swap(others, "rep", 1))
        return output(weight, parts, hidden_in)

    full_o = lax.all_gather(o_parts[0], FR, axis=0, tiled=True)
    own_cols = lax.all_to_all(
        full_o.reshape(tp, col_width, q_width), "tp", split_axis=0, concat_axis=2, tiled=True
    ).reshape(col_width, tp * q_width)
    everyone = lax.all_gather(attention, "tp", axis=0)
    everyone = everyone.reshape(tp // 2, 2, steps, half, 2, q_width)
    odd = everyone[:, 1][:, :, :, ::-1]
    everyone = jnp.stack([everyone[:, 0], odd], axis=0)
    features = everyone.transpose(2, 0, 3, 1, 4, 5).reshape(steps * rows, tp * q_width)
    mixed = jnp.dot(features, own_cols.T, preferred_element_type=F32)
    start = lax.axis_index("tp") * col_width
    residual = lax.dynamic_slice_in_dim(hidden_in, start, col_width, 2).astype(F32)
    return (residual + mixed.reshape(steps, rows, col_width)).astype(BF16)


def solution(mesh):
    placed = (
        P(None, ("fsdp", "rep"), None),
        P(),
        P("tp", None),
        P("tp"),
        P(None, "tp", None),
        P(None, "tp"),
        P(None, "tp"),
        P("tp", ("fsdp", "rep")),
        P("tp", ("fsdp", "rep")),
        P(None, "tp", ("fsdp", "rep")),
        P(None, "tp", ("fsdp", "rep")),
        P(("fsdp", "rep"), "tp"),
        P(("fsdp", "rep"), "tp"),
        P(("fsdp", "rep"), "tp", None, None),
        P(("fsdp", "rep"), "tp", None, None),
        P(("fsdp", "rep")),
    )
    return jax.shard_map(
        shards,
        mesh=mesh,
        in_specs=placed,
        out_specs=P(None, ("fsdp", "rep"), "tp"),
        check_vma=False,
    )
```

```python
import functools
import math

import jax
import jax.numpy as jnp
from jax import lax
from jax.experimental import pallas as pl
from jax.experimental.pallas import tpu as pltpu
from jax.sharding import PartitionSpec as P

HD = 128
BLOCK = 32
F32 = jnp.float32
BEGIN_MIB = 61.8
BF16 = jnp.bfloat16
FR = ("fsdp", "rep")
MB = 1 << 20


def swap(x, axis, xor):
    return lax.ppermute(x, axis, [(i, i ^ xor) for i in range(lax.axis_size(axis))])


def nt_dot(a, b):
    return lax.dot_general(a, b, (((1,), (1,)), ((), ())), preferred_element_type=F32)


def call(kernel, name, mib, weight=1024, **kw):
    return pl.pallas_call(
        kernel,
        compiler_params=pltpu.CompilerParams(vmem_limit_bytes=int(mib * MB)),
        cost_estimate=pl.CostEstimate(flops=1024, bytes_accessed=weight, transcendentals=0),
        name=name,
        **kw,
    )


def sds(shape, dtype):
    return jax.ShapeDtypeStruct(shape, dtype)


HBM = pl.BlockSpec(memory_space=pltpu.HBM)
VMEM = pl.BlockSpec(memory_space=pltpu.VMEM)
ANY = pl.BlockSpec(memory_space=pl.ANY)
DMA = pltpu.SemaphoreType.DMA


def shard_index():
    return lax.axis_index("fsdp") * lax.axis_size("rep") + lax.axis_index("rep")


def half_rows(which, half):
    return pl.multiple_of(((lax.axis_index("tp") % 2) ^ which) * half, 16)


def refreshed(base, delta, exponents):
    blocks, width = exponents.shape[0], delta.shape[1]
    factor = jnp.exp2(exponents.astype(F32)).astype(BF16)
    row = lax.broadcasted_iota(jnp.int32, (blocks, width), 0)
    col = lax.broadcasted_iota(jnp.int32, (blocks, width), 1)
    spread = jnp.where((col >> 5) == row, 1.0, 0.0).astype(BF16)
    scale = lax.dot_general(factor, spread, (((0,), (0,)), ((), ())), preferred_element_type=F32)
    return (base.astype(F32) + delta.astype(F32) * scale).astype(BF16)


def begin_kernel(
    sliced, parts, qw, kvw, ow, qd, kvd, od, kc, vc, qe, kve, oe, fresh, far, *refs
):
    outs, refs = refs[:parts], refs[parts:]
    qw_v, kvw_v, ow_v, qd_v, kvd_v, od_v, fresh_v, far_v, o_v, sem = refs
    rows, width = qd.shape
    cols = pl.ds(0 if sliced else pl.multiple_of(shard_index() * width, 128), width)
    far_rows = pl.ds(half_rows(1, far.shape[1]), far.shape[1])
    o_rows = od.shape[0]
    place = pl.ds(pl.multiple_of(shard_index() * o_rows, 16), o_rows)
    copies = []

    def copy(src, dst):
        copies.append(pltpu.make_async_copy(src, dst, sem.at[len(copies)]))
        copies[-1].start()

    copy(qw.at[:, cols], qw_v)
    copy(qd, qd_v)
    copy(kvw.at[:, :, cols], kvw_v)
    copy(kvd, kvd_v)
    copy(kc.at[far_rows], far_v.at[0])
    copy(vc.at[far_rows], far_v.at[1])
    copy(ow.at[place], ow_v)
    copy(od, od_v)
    copies[0].wait()
    copies[1].wait()
    fresh_v[:rows] = refreshed(qw_v[...], qd_v[...], qe[...])
    copy(fresh_v.at[:rows], fresh.at[:rows])
    copies[2].wait()
    copies[3].wait()
    narrow = kvd.shape[1]
    for n in range(2):
        part = slice(rows + n * narrow, rows + (n + 1) * narrow)
        fresh_v[part] = refreshed(kvw_v[n], kvd_v[n], kve[:, n, :])
    copy(fresh_v.at[rows:], fresh.at[rows:])
    copies[4].wait()
    copies[5].wait()
    copy(far_v, far)
    copies[6].wait()
    copies[7].wait()
    o_v[...] = refreshed(ow_v[...], od_v[...], oe[...])
    quarter = o_rows // 4
    if parts == 1:
        copy(o_v, outs[0])
    else:
        copy(o_v.at[:quarter], outs[0])
        copy(o_v.at[quarter : 2 * quarter], outs[1].at[:quarter])
        copy(o_v.at[3 * quarter :], outs[1].at[quarter:])
        copy(o_v.at[2 * quarter : 3 * quarter], outs[2])
    for done in copies[8:]:
        done.wait()


def begin(
    parts, q_weight, kv_weight, o_weight, q_delta, q_exp, kv_delta, kv_exp, o_delta, o_exp,
    keys, values,
):
    rows, width = q_delta.shape
    narrow = kv_delta.shape[1]
    sliced = width % 128 != 0
    if sliced:
        start = shard_index() * width
        q_weight = lax.dynamic_slice_in_dim(q_weight, start, width, 1)
        kv_weight = lax.dynamic_slice_in_dim(kv_weight, start, width, 2)
    sizes = (4,) if parts == 1 else (1, 2, 1)
    fresh = sds((rows + 2 * narrow, width), BF16)
    far = sds((2, keys.shape[0] // 2) + keys.shape[1:], BF16)
    pair = lambda a: [pltpu.VMEM(a.shape, BF16)]
    return call(
        functools.partial(begin_kernel, sliced, parts),
        "begin",
        BEGIN_MIB,
        out_shape=(fresh, far)
        + tuple(sds((o_delta.shape[0] * n // 4, o_delta.shape[1]), BF16) for n in sizes),
        in_specs=[HBM] * 8 + [VMEM] * 3,
        out_specs=(ANY,) * (2 + parts),
        scratch_shapes=(pair(q_delta) + pair(kv_delta) + pair(o_delta)) * 2
        + [pltpu.VMEM(fresh.shape, BF16), pltpu.VMEM(far.shape, BF16)]
        + pair(o_delta)
        + [DMA((15,))],
    )(
        q_weight, kv_weight, o_weight, q_delta, kv_delta, o_delta, keys, values,
        q_exp.T, kv_exp.transpose(2, 0, 1), o_exp.T,
    )


CHUNKS = 8


def prepare_kernel(hidden, gain, lengths, after, normed, cosine, sine, hidden_v, gain_v, sem):
    steps, rows, _ = hidden.shape
    tile = steps * rows // CHUNKS
    per_step = rows // tile
    loads = []
    for n in range(CHUNKS):
        s, at = n // per_step, pl.ds(n % per_step * tile, tile)
        loads.append(pltpu.make_async_copy(hidden.at[s, at], hidden_v.at[n], sem.at[n]))
    loads.append(pltpu.make_async_copy(gain, gain_v, sem.at[CHUNKS]))
    for load in loads:
        load.start()
    lane = lax.broadcasted_iota(jnp.int32, (1, HD), 1) & (HD // 2 - 1)
    frequency = jnp.exp(lane.astype(F32) * (-2.0 / HD * math.log(1000000.0)))
    length = jnp.broadcast_to(lengths[...].astype(F32), (HD, rows)).T
    low = lax.broadcasted_iota(jnp.int32, (1, HD), 1) < HD // 2
    for s in range(steps):
        angles = (length + float(s)) * frequency
        at = slice(s * rows, (s + 1) * rows)
        cosine[at] = jnp.cos(angles)
        turned = jnp.sin(angles)
        sine[at] = jnp.where(low, -turned, turned)
    loads[CHUNKS].wait()
    for n in range(CHUNKS):
        loads[n].wait()
        values = hidden_v[n].astype(F32)
        root = lax.rsqrt(jnp.mean(values * values, axis=-1, keepdims=True) + 1e-06)
        normed[n * tile : (n + 1) * tile] = (values * root * gain_v[...]).astype(BF16)


def prepare(hidden, gain, lengths, after):
    steps, rows, width = hidden.shape
    table = sds((steps * rows, HD), F32)
    return call(
        prepare_kernel,
        "prepare",
        16,
        weight=10 * MB,
        out_shape=(sds((steps * rows, width), BF16), table, table),
        in_specs=[HBM, HBM, VMEM, ANY],
        out_specs=(VMEM,) * 3,
        scratch_shapes=[
            pltpu.VMEM((CHUNKS, steps * rows // CHUNKS, width), BF16),
            pltpu.VMEM((1, width), F32),
            DMA((CHUNKS + 1,)),
        ],
    )(hidden, gain.reshape(1, width), lengths.reshape(1, rows), after)


def halves_kernel(along_x, along_y, *refs):
    first, second = refs[-2:]
    half = first.shape[0]
    first[...] = along_x[:half]
    second[...] = along_y[half:]


def halves(along_x, along_y, after):
    rows, width = along_x.shape
    out = sds((rows // 2, width), BF16)
    return call(
        halves_kernel,
        "halves",
        8,
        out_shape=(out, out),
        in_specs=[VMEM] * 2 + [ANY] * len(after),
        out_specs=(VMEM,) * 2,
    )(along_x, along_y, *after)


def term(place, normed, shard):
    width = shard.shape[1]
    owner = (lax.axis_index("fsdp") ^ place[0]) * lax.axis_size("rep")
    owner += lax.axis_index("rep") ^ place[1]
    return nt_dot(normed[:, pl.ds(pl.multiple_of(owner * width, 128), width)], shard)


def project_kernel(places, normed, *refs):
    total = term(places[0], normed, refs[0][...])
    for place, ref in zip(places[1:], refs[1:]):
        total += term(place, normed, ref[...])
    refs[-1][...] = total


def project(places, normed, shards):
    return call(
        functools.partial(project_kernel, places),
        "project",
        16,
        out_shape=sds((normed.shape[0], shards[0].shape[0]), F32),
        in_specs=[VMEM] * (1 + len(shards)),
        out_specs=VMEM,
    )(normed, *shards)


def finish_kernel(places, steps, normed, total_in, qb, kvb, cosine, sine, *refs):
    own, other, packed = refs[-3:]
    total = total_in[...]
    for n, place in enumerate(places):
        shard = refs[n][...]
        total += term(place, normed, shard)
    span = qb.shape[1]
    for head in range(span // HD):
        cols = slice(head * HD, (head + 1) * HD)
        query = total[:, cols] + qb[:, cols].astype(F32)
        turned = query * cosine[...] + pltpu.roll(query, HD // 2, 1) * sine[...]
        packed[:, cols] = turned.astype(BF16)
    key = total[:, span : span + HD // 2] + kvb[0:1].astype(F32)
    value = total[:, span + HD // 2 :] + kvb[1:2].astype(F32)
    high = key.astype(BF16)
    rest = key - high.astype(F32)
    middle = rest.astype(BF16)
    low = (rest - middle.astype(F32)).astype(BF16)
    packed[:, span : span + HD] = jnp.concatenate([high, middle], axis=1)
    packed[:, span + HD :] = jnp.concatenate([low, value.astype(BF16)], axis=1)
    rows = packed.shape[0] // steps
    for s in range(steps):
        own[s] = packed[pl.ds(s * rows + half_rows(0, rows // 2), rows // 2), :]
        other[s] = packed[pl.ds(s * rows + half_rows(1, rows // 2), rows // 2), :]


def finish(places, steps, normed, total, q_bias, kv_bias, cosine, sine, shards):
    rows = normed.shape[0] // steps
    width = q_bias.shape[0] + 2 * HD
    out = sds((steps, rows // 2, width), BF16)
    return call(
        functools.partial(finish_kernel, places, steps),
        "finish",
        16,
        out_shape=(out, out),
        in_specs=[VMEM] * (6 + len(shards)),
        out_specs=(VMEM, VMEM),
        scratch_shapes=[pltpu.VMEM((steps * rows, width), BF16)],
    )(normed, total, q_bias.reshape(1, -1), kv_bias, cosine, sine, *shards)


GROUP = 16


def attend_kernel(
    own, other, cosine, sine, swapped, lengths, keys, values,
    out, new_k, new_v, near_kv, limits, sem
):
    steps, rows, width = own.shape
    heads = (width - 2 * HD) // HD
    half = HD // 2
    parity = lax.axis_index("tp") % 2
    even = parity == 0
    first = half_rows(0, rows)
    loads = [
        pltpu.make_async_copy(src.at[pl.ds(first, rows)], near_kv.at[n], sem.at[n])
        for n, src in enumerate((keys, values))
    ]
    for load in loads:
        load.start()
    limits[...] = jnp.broadcast_to(lengths[...], (HD, lengths.shape[1])).T
    scale = HD ** (-0.5)
    base = width - 2 * HD

    def key_of(ref, s):
        top = ref[s, :, base : base + HD].astype(F32)
        rest = ref[s, :, base + HD :].astype(F32)
        return top[:, :half] + (top[:, half:] + rest[:, :half]), rest[:, half:]

    for s in range(steps):
        key_a, value_a = key_of(own, s)
        key_b, value_b = key_of(other, s)
        key = jnp.where(
            even,
            jnp.concatenate([key_a, key_b], axis=1),
            jnp.concatenate([key_b, key_a], axis=1),
        )
        value = jnp.where(
            even,
            jnp.concatenate([value_a, value_b], axis=1),
            jnp.concatenate([value_b, value_a], axis=1),
        )
        at = pl.ds(pl.multiple_of(s * 2 * rows + first, 16), rows)
        turned = key * cosine[at, :] + pltpu.roll(key, half, 1) * sine[at, :]
        new_k[s] = turned.astype(BF16)
        new_v[s] = value.astype(BF16)

    span = keys.shape[1]
    count = steps * 2 * heads * GROUP
    lane = GROUP * span
    row_of = lax.broadcasted_iota(jnp.int32, (count, lane), 0) & (GROUP - 1)
    column = lax.broadcasted_iota(jnp.int32, (count, lane), 1)
    diagonal = row_of == column // span
    slot = column % span
    fresh = GROUP * steps
    fresh_row = lax.broadcasted_iota(jnp.int32, (count, fresh), 0)
    fresh_col = lax.broadcasted_iota(jnp.int32, (count, fresh), 1)
    fresh_ok = jnp.logical_and(
        (fresh_row & (GROUP - 1)) == (fresh_col & (GROUP - 1)),
        fresh_col // GROUP <= fresh_row // (2 * heads * GROUP),
    )
    lowest = -1e30
    for load in loads:
        load.wait()
    for g in range(rows // GROUP):
        at = slice(g * GROUP, (g + 1) * GROUP)
        query = jnp.concatenate(
            [
                ref[s, at, h * HD : (h + 1) * HD]
                for s in range(steps)
                for ref in (own, other)
                for h in range(heads)
            ],
            axis=0,
        )
        near_k = near_kv[0, at].reshape(lane, HD)
        near_v = near_kv[1, at].reshape(lane, HD)
        far_k = swapped[0, at].reshape(lane, HD)
        far_v = swapped[1, at].reshape(lane, HD)
        fresh_k = jnp.concatenate([new_k[s, at] for s in range(steps)], axis=0)
        fresh_v = jnp.concatenate([new_v[s, at] for s in range(steps)], axis=0)
        limit = limits[pl.ds(first + g * GROUP, GROUP), :1]
        limit = jnp.concatenate([limit] * (count // GROUP), axis=0)
        ok_n = jnp.logical_and(diagonal, slot + parity * span < limit)
        ok_f = jnp.logical_and(diagonal, slot + (1 - parity) * span < limit)
        score_n = jnp.where(ok_n, nt_dot(query, near_k) * scale, lowest)
        score_f = jnp.where(ok_f, nt_dot(query, far_k) * scale, lowest)
        score_x = jnp.where(fresh_ok, nt_dot(query, fresh_k) * scale, lowest)
        top_n = jnp.max(score_n, axis=1, keepdims=True)
        top_f = jnp.max(score_f, axis=1, keepdims=True)
        top_x = jnp.max(score_x, axis=1, keepdims=True)
        top_n = jnp.where(even, jnp.maximum(top_n, top_x), top_n)
        top_f = jnp.where(even, top_f, jnp.maximum(top_f, top_x))
        top_x = jnp.where(even, top_n, top_f)
        weight_n = jnp.where(ok_n, jnp.exp(score_n - top_n), 0.0)
        weight_f = jnp.where(ok_f, jnp.exp(score_f - top_f), 0.0)
        weight_x = jnp.where(fresh_ok, jnp.exp(score_x - top_x), 0.0)
        top_all = jnp.maximum(top_n, top_f)
        factor_n = jnp.exp(top_n - top_all)
        factor_f = jnp.exp(top_f - top_all)
        factor_x = jnp.where(even, factor_n, factor_f)
        acc = (
            factor_n * jnp.dot(weight_n.astype(BF16), near_v, preferred_element_type=F32)
            + factor_f * jnp.dot(weight_f.astype(BF16), far_v, preferred_element_type=F32)
            + factor_x * jnp.dot(weight_x.astype(BF16), fresh_v, preferred_element_type=F32)
        )
        total = (
            factor_n * jnp.sum(weight_n, axis=1, keepdims=True)
            + factor_f * jnp.sum(weight_f, axis=1, keepdims=True)
            + factor_x * jnp.sum(weight_x, axis=1, keepdims=True)
        )
        result = (acc / total).astype(BF16)
        for s in range(steps):
            for h in range(2 * heads):
                place = (s * 2 * heads + h) * GROUP
                out[s, at, h * HD : (h + 1) * HD] = result[place : place + GROUP]


def attend(own, other, cosine, sine, swapped, lengths, keys, values):
    steps, rows, width = own.shape
    return call(
        attend_kernel,
        "attend",
        24,
        out_shape=sds((steps, rows, 2 * (width - 2 * HD)), BF16),
        in_specs=[VMEM] * 6 + [HBM] * 2,
        out_specs=VMEM,
        scratch_shapes=[
            pltpu.VMEM((steps, rows, HD), BF16),
            pltpu.VMEM((steps, rows, HD), BF16),
            pltpu.VMEM((2, rows) + keys.shape[1:], BF16),
            pltpu.VMEM((lengths.shape[0], HD), jnp.int32),
            DMA((2,)),
        ],
    )(own, other, cosine, sine, swapped, lengths.reshape(1, -1), keys, values)


def relay_kernel(own, along_x, *refs):
    out = refs[-1]
    rows = own.shape[0]
    out[:rows] = own[...]
    out[rows:] = along_x[rows:]


def relay(own, along_x, after):
    return call(
        relay_kernel,
        "relay",
        8,
        out_shape=sds(along_x.shape, BF16),
        in_specs=[VMEM] * 2 + [ANY] * len(after),
        out_specs=VMEM,
    )(own, along_x, *after)


def pick_kernel(own, along_x, along_y, *refs):
    outs, rows = refs[-4:], own.shape[0]
    blocks = [own[...], along_x[:rows], along_y[:rows], along_y[rows:]]
    where = lax.axis_index("fsdp") ^ lax.axis_index("tp")
    for k, out in enumerate(outs):
        for i, block in enumerate(blocks):

            @pl.when((where ^ k) == i)
            def _(out=out, block=block):
                out[...] = block


def pick(own, along_x, along_y, after):
    return call(
        pick_kernel,
        "pick",
        8,
        out_shape=(sds(own.shape, BF16),) * 4,
        in_specs=[VMEM] * 3 + [ANY] * len(after),
        out_specs=(VMEM,) * 4,
    )(own, along_x, along_y, *after)


def stack_kernel(*refs):
    place = 0
    for ref in refs[:-1]:
        rows = ref.shape[0]
        if place < refs[-1].shape[0]:
            refs[-1][place : place + rows] = ref[...]
        place += rows


def stack(blocks, after):
    rows, width = sum(b.shape[0] for b in blocks), blocks[0].shape[1]
    return call(
        stack_kernel,
        "stack",
        8,
        out_shape=sds((rows, width), BF16),
        in_specs=[VMEM] * len(blocks) + [ANY] * len(after),
        out_specs=VMEM,
    )(*blocks, *after)


def assemble_kernel(*refs):
    weight = refs[-1]
    count = (len(refs) - 1) // 2
    rows, width = refs[0].shape[0] // 4, refs[0].shape[1]
    for j in range(2):
        shards = refs[j * count : (j + 1) * count]
        blocks = [(ref, n * 4) for ref in shards for n in range(ref.shape[0] // (4 * rows))]
        for i, (shard, first) in enumerate(blocks):
            quarter = lax.axis_index("fsdp") ^ i ^ lax.axis_index("tp")
            place = ((lax.axis_index("rep") ^ j) * 4 + quarter) * rows
            for k in range(4):
                weight[pl.ds(pl.multiple_of(place, 16), rows), k * width : (k + 1) * width] = (
                    shard[(first + k) * rows : (first + k + 1) * rows]
                )


def assemble(own, across):
    rows, width = own[0].shape
    shards = [*own, *across]
    return call(
        assemble_kernel,
        "assemble",
        16,
        out_shape=sds((2 * rows, 4 * width), BF16),
        in_specs=[VMEM] * len(shards),
        out_specs=VMEM,
    )(*shards)


def output_kernel(weight, a0, a1, a2, a3, hidden, out, hidden_v, out_v, load_sem, store_sem):
    width = weight.shape[1] // 4
    steps, half = a0.shape[:2]
    cols = out.shape[2]
    place = pl.ds(pl.multiple_of(lax.axis_index("tp") * cols, 128), cols)
    load = pltpu.make_async_copy(hidden.at[:, :, place], hidden_v, load_sem)
    load.start()
    flat = lambda ref: ref[...].reshape(steps * half, 2 * width)
    turned = lambda ref: jnp.concatenate([flat(ref)[:, width:], flat(ref)[:, :width]], axis=1)
    near = jnp.concatenate([flat(a0), flat(a2)], axis=1)
    far = jnp.concatenate([turned(a1), turned(a3)], axis=1)
    features = jnp.concatenate([near, far], axis=0)
    tile = cols // store_sem.shape[0]
    stores = []
    for n in range(store_sem.shape[0]):
        part = slice(n * tile, (n + 1) * tile)
        total = nt_dot(features, weight[part])
        if n == 0:
            load.wait()
        for which in range(2):
            for s in range(steps):
                at = pl.ds(half_rows(which, half), half)
                first = (which * steps + s) * half
                mixed = total[first : first + half]
                out_v[s, at, part] = (hidden_v[s, at, part].astype(F32) + mixed).astype(BF16)
        stores.append(
            pltpu.make_async_copy(out_v.at[:, :, part], out.at[:, :, part], store_sem.at[n])
        )
        stores[-1].start()
    for store in stores:
        store.wait()


def output(weight, parts, hidden):
    steps, rows, _ = hidden.shape
    shape = (steps, rows, weight.shape[0])
    return call(
        output_kernel,
        "output",
        24,
        out_shape=sds(shape, BF16),
        in_specs=[VMEM] * (1 + len(parts)) + [HBM],
        out_specs=ANY,
        scratch_shapes=[
            pltpu.VMEM(shape, BF16),
            pltpu.VMEM(shape, BF16),
            DMA,
            DMA((max(1, shape[2] // 256),)),
        ],
    )(weight, *parts, hidden)


def shards(
    hidden_in,
    norm_gain,
    q_weight,
    q_bias,
    kv_weight,
    kv_bias,
    o_weight,
    q_delta,
    q_scale_exp,
    kv_delta,
    kv_scale_exp,
    o_delta,
    o_scale_exp,
    key_cache,
    value_cache,
    cache_lengths,
):
    steps, rows, model_width = hidden_in.shape
    q_width = q_weight.shape[0]
    half = rows // 2
    fsdp, tp, rep = (lax.axis_size(a) for a in ("fsdp", "tp", "rep"))
    shard_width = q_delta.shape[1]
    col_width = model_width // tp
    small = fsdp == 4 and tp == 4 and rep == 2 and shard_width % 128 == 0 and col_width % 128 == 0
    keys, values = key_cache[:, 0], value_cache[:, 0]

    fresh, far, *o_parts = begin(
        3 if small else 1, q_weight, kv_weight, o_weight, q_delta, q_scale_exp, kv_delta,
        kv_scale_exp, o_delta, o_scale_exp, keys, values,
    )
    swapped = swap(far, "tp", 1)
    normed, cosine, sine = prepare(hidden_in, norm_gain, cache_lengths, o_parts[0])

    if small:
        along_x, along_y = swap(fresh, "fsdp", 1), swap(fresh, "fsdp", 2)
        o_x = swap(o_parts[1], "fsdp", 1)
        first, second = halves(along_x, along_y, [cosine])
        last = stack([swap(first, "fsdp", 2), swap(second, "fsdp", 1)], [])
        o_y = swap(relay(o_parts[2], o_x, [first]), "fsdp", 2)
        near = [fresh, along_x, along_y]
        near += [swap(a, "rep", 1) for a in near]
        total = project([(i, j) for j in (0, 1) for i in (0, 1, 2)], normed, near)
        last = [last, swap(last, "rep", 1)]
        own, other = finish(
            [(3, 0), (3, 1)], steps, normed, total, q_bias, kv_bias, cosine, sine, last
        )
    else:
        full = lax.all_gather(fresh, FR, axis=1, tiled=True)
        total = jnp.dot(normed, full.T, preferred_element_type=F32)
        own, other = finish([], steps, normed, total, q_bias, kv_bias, cosine, sine, [])

    received = swap(other, "tp", 1)
    attention = attend(own, received, cosine, sine, swapped, cache_lengths, keys, values)

    if small:
        picked = pick(o_parts[0], o_x, o_y, [swapped])
        blocks = [picked[0]] + [swap(picked[k], "tp", k) for k in (1, 2, 3)]
        stacked = stack(blocks, [own])
        parts = [attention] + [swap(attention, "tp", k) for k in (1, 2, 3)]
        others = stack([swap(stacked, "fsdp", i) for i in (1, 2, 3)], parts[1:])
        weight = assemble([stacked, others], [swap(stacked, "rep", 1), swap(others, "rep", 1)])
        return output(weight, parts, hidden_in)

    full_o = lax.all_gather(o_parts[0], FR, axis=0, tiled=True)
    own_cols = lax.all_to_all(
        full_o.reshape(tp, col_width, q_width), "tp", split_axis=0, concat_axis=2, tiled=True
    ).reshape(col_width, tp * q_width)
    everyone = lax.all_gather(attention, "tp", axis=0)
    everyone = everyone.reshape(tp // 2, 2, steps, half, 2, q_width)
    odd = everyone[:, 1][:, :, :, ::-1]
    everyone = jnp.stack([everyone[:, 0], odd], axis=0)
    features = everyone.transpose(2, 0, 3, 1, 4, 5).reshape(steps * rows, tp * q_width)
    mixed = jnp.dot(features, own_cols.T, preferred_element_type=F32)
    start = lax.axis_index("tp") * col_width
    residual = lax.dynamic_slice_in_dim(hidden_in, start, col_width, 2).astype(F32)
    return (residual + mixed.reshape(steps, rows, col_width)).astype(BF16)


def solution(mesh):
    placed = (
        P(None, ("fsdp", "rep"), None),
        P(),
        P("tp", None),
        P("tp"),
        P(None, "tp", None),
        P(None, "tp"),
        P(None, "tp"),
        P("tp", ("fsdp", "rep")),
        P("tp", ("fsdp", "rep")),
        P(None, "tp", ("fsdp", "rep")),
        P(None, "tp", ("fsdp", "rep")),
        P(("fsdp", "rep"), "tp"),
        P(("fsdp", "rep"), "tp"),
        P(("fsdp", "rep"), "tp", None, None),
        P(("fsdp", "rep"), "tp", None, None),
        P(("fsdp", "rep")),
    )
    return jax.shard_map(
        shards,
        mesh=mesh,
        in_specs=placed,
        out_specs=P(None, ("fsdp", "rep"), "tp"),
        check_vma=False,
    )
```
